512 devices in a mesh: user: 32 (over z, x), tensor: 16 (over y, core).
Axes of the slice: x: 4, y: 8, z: 8, core: 2. Of those that a mesh axis runs over, the one named last changes fastest.
Arguments:
- activations: bfloat16 [2, 24576, 8192], P(None, 'user', 'tensor'), may hold values from -70 to 70, as said below
- key_grads: bfloat16 [2, 24576, 1024], P(None, 'user'), may hold values from -2.4 to 2.4
- row_users: int32 [2, 24576], P(None, 'user'), may hold values from 0 to 7, as said below
Outputs:
- clipped_mean: float32 [1024, 8192], P('user', 'tensor')
The draws below stay inside these ranges and needn't reach their ends.
Inputs may be any that keep to these rules, and one draw needn't show every extreme that they name: `activations`: activations are finite. `row_users`: every aligned block of 768 rows names every user 0 to 7 at least once.
All inputs are finite; a program needn't handle non-finite values.
Results may differ from the reference program's by a relative error of at most 0.0012.
Values sent between devices are 32-bit elements; how exact they have to be, the bound alone decides.
No kernel may reach another device: no remote copies, remote signals or barrier semaphores. Data moves between devices by JAX's collectives and lax.ppermute only.
A program may use at most 64 MiB of HBM per device.

```python
import math
import jax
import jax.numpy as jnp
from jax import lax

D = 8192
KV = 1024
MICRO = 2
ROWS = 768
USERS_MB = 8
ROWS_ALL = 24576
BLOCKS = 64
N_USER = 32


def user_layout(key):
    key = jax.random.fold_in(key, 23)
    first_key, second_key = jax.random.split(key)
    weights = jax.random.randint(first_key, (BLOCKS, USERS_MB), 1, 17, dtype=jnp.int32)
    spare = ROWS - USERS_MB
    bounds = jnp.cumsum(weights, axis=1) * spare // jnp.sum(weights, axis=1, keepdims=True)
    previous = jnp.concatenate([jnp.zeros((BLOCKS, 1), jnp.int32), bounds[:, :-1]], axis=1)
    counts = 1 + bounds - previous
    ends = jnp.cumsum(counts, axis=1)
    position = jnp.arange(ROWS, dtype=jnp.int32)
    sorted_users = jnp.sum((ends[:, :, None] <= position[None, None, :]).astype(jnp.int32), axis=1)
    scores = jax.random.randint(second_key, (BLOCKS, ROWS), 0, 1048576, dtype=jnp.int32) * ROWS + position[None, :]
    order = jnp.argsort(scores, axis=1, stable=True)
    return jnp.take_along_axis(sorted_users, order, axis=1).astype(jnp.int32)


def spread_users(common, owners):
    return jax.vmap(lambda table, index: table[index])(common, owners)


def draw_row_users(key, part):
    return user_layout(key).reshape(MICRO, ROWS_ALL).astype(jnp.int32)


def draw_activations(key, part):
    owners = user_layout(key)
    key = jax.random.fold_in(key, 11)
    first_key, second_key, third_key, fourth_key = jax.random.split(key, 4)
    column = jnp.arange(D, dtype=jnp.float32) / D
    ramp = jnp.sqrt(1.0 + 2.0 * column)
    share = 0.5
    own = jax.random.normal(first_key, (BLOCKS, ROWS, D), jnp.float32)
    common = jax.random.normal(fourth_key, (BLOCKS, USERS_MB, D), jnp.float32)
    mixed = share * spread_users(common, owners) + (1.0 - share * share) ** 0.5 * own
    mixed = jnp.clip(mixed, -6.0, 6.0)
    column_scale = ramp * jnp.exp(jax.random.uniform(second_key, (D,), jnp.float32, -1.15, 1.15))
    row_scale = jnp.exp(jax.random.uniform(third_key, (BLOCKS, ROWS, 1), jnp.float32, -0.7, 0.7))
    values = mixed * column_scale * row_scale
    return values.reshape(MICRO, ROWS_ALL, D).astype(jnp.bfloat16)


def draw_key_grads(key, part):
    owners = user_layout(key)
    key = jax.random.fold_in(key, 37)
    first_key, second_key, third_key = jax.random.split(key, 3)
    share = 0.5
    scale = 0.1
    own = jax.random.normal(first_key, (BLOCKS, ROWS, KV), jnp.float32)
    common = jax.random.normal(second_key, (BLOCKS, USERS_MB, KV), jnp.float32)
    mixed = share * spread_users(common, owners) + (1.0 - share * share) ** 0.5 * own
    mixed = jnp.clip(mixed, -8.0, 8.0)
    groups = ROWS_ALL // ROWS
    pairing = jax.random.permutation(third_key, groups)
    row_block = jnp.arange(ROWS_ALL, dtype=jnp.int32) // ROWS
    column_block = jnp.arange(KV, dtype=jnp.int32) // (KV // groups)
    boost = jnp.where(column_block[None, :] == pairing[row_block][:, None], 3.0, 1.0).astype(jnp.float32)
    values = mixed.reshape(MICRO, ROWS_ALL, KV) * scale * boost[None, :, :]
    return values.astype(jnp.bfloat16)


def setup_inputs(seed: int = 0) -> dict:
    seeds = jax.random.split(jax.random.key(seed), 4)
    activations = draw_activations(jax.random.fold_in(seeds[3], 71), 0)
    key_grads = draw_key_grads(jax.random.fold_in(seeds[3], 71), 0)
    row_users = draw_row_users(jax.random.fold_in(seeds[3], 71), 0)
    return {"activations": activations, "key_grads": key_grads, "row_users": row_users}


def block_norms(inputs, gradient, owners):
    xgram = jnp.dot(inputs, inputs.T, preferred_element_type=jnp.float32)
    ggram = jnp.dot(gradient, gradient.T, preferred_element_type=jnp.float32)
    table = (owners[None, :] == jnp.arange(USERS_MB, dtype=jnp.int32)[:, None]).astype(jnp.float32)
    spread = jnp.dot(table, xgram * ggram, precision=lax.Precision.HIGHEST)
    return lax.optimization_barrier(jnp.sum(spread * table, axis=1))

def reference(activations, key_grads, row_users):
    blocks = MICRO * N_USER
    inputs = activations.reshape(blocks, ROWS, D)
    gradient = key_grads.reshape(blocks, ROWS, KV)
    owners = row_users.reshape(blocks, ROWS).astype(jnp.int32)
    squares = lax.map(lambda item: block_norms(item[0], item[1], item[2]), (inputs, gradient, owners))
    bound = 0.3 * math.sqrt(D * KV * ROWS / USERS_MB)
    factor = bound / jnp.maximum(jnp.sqrt(squares), bound)
    row_factor = jnp.take_along_axis(factor, owners, axis=1)
    weighted = (gradient.astype(jnp.float32) * row_factor[:, :, None]).astype(jnp.bfloat16)
    total = lax.dot_general(weighted.reshape(blocks * ROWS, KV), inputs.reshape(blocks * ROWS, D), (((0,), (0,)), ((), ())), preferred_element_type=jnp.float32)
    return total / (MICRO * N_USER * USERS_MB)
```

```python
import math

import jax
import jax.numpy as jnp
from jax import lax
from jax.sharding import Mesh, PartitionSpec as P

D = 8192
KV = 1024
ROWS = 768
USERS_MB = 8
NZ, NX, NY, NC = 8, 4, 8, 2


def user_table(owners):
    labels = lax.broadcasted_iota(jnp.int32, (USERS_MB, owners.shape[0]), 0)
    return (owners[None, :] == labels).astype(jnp.float32)


def local_norms(inputs, gradient, owners):
    xgram = jnp.dot(inputs, inputs.T, preferred_element_type=jnp.float32)
    ggram = jnp.dot(gradient, gradient.T, preferred_element_type=jnp.float32)
    table = user_table(owners)
    spread = jnp.dot(table, xgram * ggram, precision=lax.Precision.HIGHEST)
    return jnp.sum(spread * table, axis=1)


def clip_rows(gradient, owners, squares, bound):
    factor = bound / jnp.maximum(jnp.sqrt(squares), bound)
    row_factor = jnp.sum(user_table(owners) * factor[:, None], axis=0)
    return (gradient.astype(jnp.float32) * row_factor[:, None]).astype(jnp.bfloat16)


def body(activations, key_grads, row_users):
    batches = activations.shape[0]
    bound = 0.3 * math.sqrt(D * KV * ROWS / USERS_MB)
    partial = jnp.stack([
        local_norms(activations[m], key_grads[m], row_users[m]) for m in range(batches)
    ])
    shared = NY * NC
    spread = jnp.broadcast_to(partial[None], (shared,) + partial.shape)
    squares = jnp.sum(lax.all_to_all(spread, ("y", "core"), 0, 0), axis=0)
    weighted = jnp.stack([
        clip_rows(key_grads[m], row_users[m], squares[m], bound) for m in range(batches)
    ])
    total = lax.dot_general(
        weighted.reshape(batches * ROWS, KV),
        activations.reshape(batches * ROWS, -1),
        (((0,), (0,)), ((), ())),
        preferred_element_type=jnp.float32,
    ) * (1.0 / (batches * NZ * NX * USERS_MB))
    width = total.shape[1]
    rows = KV // (NZ * NX)
    total = total.reshape(NZ, NX, rows, width).swapaxes(0, 1)
    total = jnp.sum(lax.all_to_all(total, "x", 0, 0), axis=0)
    return jnp.sum(lax.all_to_all(total, "z", 0, 0), axis=0)


def solution(mesh):
    split = Mesh(mesh.devices.reshape(NZ, NX, NY, NC), ("z", "x", "y", "core"))
    user, tensor = ("z", "x"), ("y", "core")
    return jax.shard_map(
        body,
        mesh=split,
        in_specs=(P(None, user, tensor), P(None, user, None), P(None, user)),
        out_specs=P(user, tensor),
        check_vma=False,
    )
```

```python
import math

import jax
import jax.numpy as jnp
from jax import lax
from jax.experimental import pallas as pl
from jax.experimental.pallas import tpu as pltpu
from jax.sharding import Mesh, PartitionSpec as P

D = 8192
KV = 1024
MICRO = 2
ROWS = 768
USERS_MB = 8
NZ, NX, NY, NC = 8, 4, 8, 2
NU, NT = NZ * NX, NY * NC
WIDTH = D // NT
OUT = KV // NU
TILE = 256
BOUND = 0.3 * math.sqrt(D * KV * ROWS / USERS_MB)
NT_DIMS = (((1,), (1,)), ((), ()))
VMEM_BYTES = 40 * 1024 * 1024


def norms_kernel(x_ref, g_ref, u_ref, out_ref):
    micro = pl.program_id(0)
    users = u_ref[pl.ds(micro, 1), :]
    columns = jnp.transpose(jnp.broadcast_to(users, (8, ROWS)))
    tiles = ROWS // TILE
    sums = [jnp.zeros((1, TILE), jnp.float32) for _ in range(tiles)]
    for i in range(tiles):
        left = pl.ds(i * TILE, TILE)
        for j in range(i, tiles):
            right = pl.ds(j * TILE, TILE)
            xgram = lax.dot_general(x_ref[0, left, :], x_ref[0, right, :], NT_DIMS, preferred_element_type=jnp.float32)
            ggram = lax.dot_general(g_ref[0, left, :], g_ref[0, right, :], NT_DIMS, preferred_element_type=jnp.float32)
            same = columns[i * TILE:(i + 1) * TILE, :1] == users[:, j * TILE:(j + 1) * TILE]
            part = jnp.sum(jnp.where(same, xgram * ggram, 0.0), axis=0, keepdims=True)
            sums[j] = sums[j] + (part if i == j else 2.0 * part)
    total = jnp.concatenate(sums, axis=1)
    labels = lax.broadcasted_iota(jnp.int32, (USERS_MB, ROWS), 0)
    squares = jnp.sum(jnp.where(users == labels, total, 0.0), axis=1, keepdims=True)
    lanes = lax.broadcasted_iota(jnp.int32, (USERS_MB, 128), 1)
    placed = jnp.where(lanes == micro, squares, 0.0)

    @pl.when(micro == 0)
    def _():
        out_ref[...] = jnp.broadcast_to(placed[None], out_ref.shape)

    @pl.when(micro != 0)
    def _():
        out_ref[...] += jnp.broadcast_to(placed[None], out_ref.shape)


def local_norms(activations, key_grads, row_users):
    return pl.pallas_call(
        norms_kernel,
        grid=(MICRO,),
        in_specs=[
            pl.BlockSpec((1, ROWS, WIDTH), lambda m: (m, 0, 0)),
            pl.BlockSpec((1, ROWS, KV), lambda m: (m, 0, 0)),
            pl.BlockSpec((MICRO, ROWS), lambda m: (0, 0)),
        ],
        out_specs=pl.BlockSpec((NT, USERS_MB, 128), lambda m: (0, 0, 0)),
        out_shape=jax.ShapeDtypeStruct((NT, USERS_MB, 128), jnp.float32),
        compiler_params=pltpu.CompilerParams(vmem_limit_bytes=VMEM_BYTES),
        name="norms",
    )(activations, key_grads, row_users)


def flip_kernel(g_ref, out_ref):
    flipped = jnp.transpose(g_ref[0])
    for x in range(NX):
        out_ref[x, 0] = flipped[x * OUT:(x + 1) * OUT, :]


def flip(key_grads):
    return pl.pallas_call(
        flip_kernel,
        grid=(MICRO, NZ),
        in_specs=[pl.BlockSpec((1, ROWS, NX * OUT), lambda m, z: (m, 0, z))],
        out_specs=pl.BlockSpec((NX, 1, OUT, ROWS), lambda m, z: (0, z, 0, m)),
        out_shape=jax.ShapeDtypeStruct((NX, NZ, OUT, MICRO * ROWS), jnp.bfloat16),
        compiler_params=pltpu.CompilerParams(vmem_limit_bytes=VMEM_BYTES),
        name="flip",
    )(key_grads)


def grad_kernel(gt_ref, x_ref, u_ref, sq_ref, out_ref, factor_ref):
    @pl.when(pl.program_id(0) == 0)
    def _():
        squares = jnp.sum(sq_ref[...], axis=0)
        factor = BOUND / jnp.maximum(jnp.sqrt(squares), BOUND)
        labels = lax.broadcasted_iota(jnp.int32, (USERS_MB, ROWS), 0)
        for m in range(MICRO):
            mine = u_ref[m:m + 1, :] == labels
            rows = jnp.sum(jnp.where(mine, factor[:, m:m + 1], 0.0), axis=0, keepdims=True)
            factor_ref[:, m * ROWS:(m + 1) * ROWS] = rows

    gt = gt_ref[0].reshape(NZ * OUT, MICRO * ROWS)
    weighted = (gt.astype(jnp.float32) * factor_ref[...]).astype(jnp.bfloat16)
    total = jnp.dot(weighted, x_ref[...], preferred_element_type=jnp.float32)
    out_ref[0] = total * (1.0 / (MICRO * NU * USERS_MB))


def clipped_grad(flipped, activations, row_users, squares):
    return pl.pallas_call(
        grad_kernel,
        grid=(NX,),
        in_specs=[
            pl.BlockSpec((1, NZ, OUT, MICRO * ROWS), lambda x: (x, 0, 0, 0)),
            pl.BlockSpec((MICRO * ROWS, WIDTH), lambda x: (0, 0)),
            pl.BlockSpec((MICRO, ROWS), lambda x: (0, 0)),
            pl.BlockSpec((NT, USERS_MB, 128), lambda x: (0, 0, 0)),
        ],
        out_specs=pl.BlockSpec((1, NZ * OUT, WIDTH), lambda x: (x, 0, 0)),
        out_shape=jax.ShapeDtypeStruct((NX, NZ * OUT, WIDTH), jnp.float32),
        scratch_shapes=[pltpu.VMEM((1, MICRO * ROWS), jnp.float32)],
        compiler_params=pltpu.CompilerParams(vmem_limit_bytes=VMEM_BYTES),
        name="grad",
    )(flipped, activations.reshape(MICRO * ROWS, WIDTH), row_users, squares)


def body(activations, key_grads, row_users):
    partial = local_norms(activations, key_grads, row_users)
    squares = lax.all_to_all(partial, ("y", "core"), 0, 0)
    flipped = flip(key_grads)
    total = clipped_grad(flipped, activations, row_users, squares)
    total = jnp.sum(lax.all_to_all(total, "x", 0, 0), axis=0)
    total = total.reshape(NZ, OUT, WIDTH)
    return jnp.sum(lax.all_to_all(total, "z", 0, 0), axis=0)


def solution(mesh):
    split = Mesh(mesh.devices.reshape(NZ, NX, NY, NC), ("z", "x", "y", "core"))
    user, tensor = ("z", "x"), ("y", "core")
    return jax.shard_map(
        body,
        mesh=split,
        in_specs=(P(None, user, tensor), P(None, user, None), P(None, user)),
        out_specs=P(user, tensor),
        check_vma=False,
    )
```

```python
import math

import jax
import jax.numpy as jnp
from jax import lax
from jax.experimental import pallas as pl
from jax.experimental.pallas import tpu as pltpu
from jax.sharding import Mesh, PartitionSpec as P

D = 8192
KV = 1024
MICRO = 2
ROWS = 768
USERS_MB = 8
NZ, NX, NY, NC = 8, 4, 8, 2
NU, NT = NZ * NX, NY * NC
PAIRS = ((0, 1), (3, 2))
CLASSES = ((0, 3), (1, 2))
MEMBERS, DESTS = 4, 8
WIDTH = D // NT
OUT = KV // NU
TILE = 256
BOUND = 0.3 * math.sqrt(D * KV * ROWS / USERS_MB)
NT_DIMS = (((1,), (1,)), ((), ()))
VMEM_BYTES = 60 * 1024 * 1024


def norms_kernel(x_hbm, g_hbm, u_ref, out_ref, x_ref, g_ref, gram_ref, sems):
    tiles = ROWS // TILE
    copies = []
    for m in range(MICRO):
        copies.append((
            pltpu.make_async_copy(g_hbm.at[m], g_ref.at[m], sems.at[0, m]),
            pltpu.make_async_copy(x_hbm.at[m], x_ref.at[m], sems.at[1, m]),
        ))
        for copy in copies[m]:
            copy.start()
    pairs = [(i, j) for j in range(tiles) for i in range(j + 1)]
    placed = jnp.zeros((USERS_MB, 128), jnp.float32)
    for m in range(MICRO):
        users = u_ref[m:m + 1, :]
        columns = jnp.transpose(jnp.broadcast_to(users, (8, ROWS)))
        copies[m][0].wait()
        for at, (i, j) in enumerate(pairs):
            left, right = pl.ds(i * TILE, TILE), pl.ds(j * TILE, TILE)
            ggram = lax.dot_general(g_ref[m, left, :], g_ref[m, right, :], NT_DIMS, preferred_element_type=jnp.float32)
            same = columns[i * TILE:(i + 1) * TILE, :1] == users[:, j * TILE:(j + 1) * TILE]
            gram_ref[at] = jnp.where(same, ggram if i == j else 2.0 * ggram, 0.0)
        copies[m][1].wait()
        sums = [jnp.zeros((1, TILE), jnp.float32) for _ in range(tiles)]
        for at, (i, j) in enumerate(pairs):
            left, right = pl.ds(i * TILE, TILE), pl.ds(j * TILE, TILE)
            xgram = lax.dot_general(x_ref[m, left, :], x_ref[m, right, :], NT_DIMS, preferred_element_type=jnp.float32)
            sums[j] = sums[j] + jnp.sum(xgram * gram_ref[at], axis=0, keepdims=True)
        total = jnp.concatenate(sums, axis=1)
        labels = lax.broadcasted_iota(jnp.int32, (USERS_MB, ROWS), 0)
        squares = jnp.sum(jnp.where(users == labels, total, 0.0), axis=1, keepdims=True)
        lanes = lax.broadcasted_iota(jnp.int32, (USERS_MB, 128), 1)
        placed = placed + jnp.where(lanes == m, squares, 0.0)
    out_ref[...] = jnp.broadcast_to(placed[None], out_ref.shape)


def local_norms(activations, key_grads, row_users):
    return pl.pallas_call(
        norms_kernel,
        in_specs=[
            pl.BlockSpec(memory_space=pltpu.HBM),
            pl.BlockSpec(memory_space=pltpu.HBM),
            pl.BlockSpec(memory_space=pltpu.VMEM),
        ],
        out_specs=pl.BlockSpec(memory_space=pltpu.VMEM),
        out_shape=jax.ShapeDtypeStruct((NT, USERS_MB, 128), jnp.float32),
        scratch_shapes=[
            pltpu.VMEM((MICRO, ROWS, WIDTH), jnp.bfloat16),
            pltpu.VMEM((MICRO, ROWS, KV), jnp.bfloat16),
            pltpu.VMEM((6, TILE, TILE), jnp.float32),
            pltpu.SemaphoreType.DMA((2, MICRO)),
        ],
        compiler_params=pltpu.CompilerParams(vmem_limit_bytes=VMEM_BYTES),
        name="norms",
    )(activations, key_grads, row_users)


def flip_kernel(core_ref, g_hbm, out_hbm, g_ref, out_ref, sems):
    core = core_ref[0]
    reads = [pltpu.make_async_copy(g_hbm.at[m], g_ref.at[m], sems.at[0, m]) for m in range(MICRO)]
    writes = [pltpu.make_async_copy(out_ref.at[k], out_hbm.at[k], sems.at[1, k]) for k in range(MEMBERS)]
    for copy in reads:
        copy.start()
    for m in range(MICRO):
        reads[m].wait()
        for z in range(NZ):
            flipped = jnp.transpose(g_ref[m, :, z * NX * OUT:(z + 1) * NX * OUT])
            zc = lax.rem(z + NZ - core, NZ)
            for x in range(NX):
                xc = lax.rem(x + NX - core, NX)
                inner = jnp.where((xc == 0) | (xc == 3), 0, 1)
                member = 2 * lax.rem(zc, 2) + inner
                dest = 2 * (zc // 2) + xc // 2
                out_ref[member, dest, :, m * ROWS:(m + 1) * ROWS] = flipped[x * OUT:(x + 1) * OUT, :]
    for copy in writes:
        copy.start()
    for copy in writes:
        copy.wait()


def flip(core, key_grads):
    shape = (MEMBERS, DESTS, OUT, MICRO * ROWS)
    return pl.pallas_call(
        flip_kernel,
        in_specs=[pl.BlockSpec(memory_space=pltpu.SMEM), pl.BlockSpec(memory_space=pltpu.HBM)],
        out_specs=pl.BlockSpec(memory_space=pltpu.HBM),
        out_shape=jax.ShapeDtypeStruct(shape, jnp.bfloat16),
        scratch_shapes=[
            pltpu.VMEM((MICRO, ROWS, KV), jnp.bfloat16),
            pltpu.VMEM(shape, jnp.bfloat16),
            pltpu.SemaphoreType.DMA((2, MEMBERS)),
        ],
        compiler_params=pltpu.CompilerParams(vmem_limit_bytes=VMEM_BYTES),
        name="flip",
    )(core, key_grads)


def grad_kernel(gt_hbm, x_hbm, u_ref, sq_ref, out_hbm, gt_ref, x_ref, factor_ref, out_ref, sems):
    inputs = pltpu.make_async_copy(x_hbm, x_ref, sems.at[0, MEMBERS])
    parts = [pltpu.make_async_copy(gt_hbm.at[k], gt_ref.at[k], sems.at[0, k]) for k in range(MEMBERS)]
    writes = [pltpu.make_async_copy(out_ref.at[k], out_hbm.at[k], sems.at[1, k]) for k in range(MEMBERS)]
    inputs.start()
    for copy in parts:
        copy.start()
    squares = jnp.sum(sq_ref[...], axis=0)
    factor = BOUND / jnp.maximum(jnp.sqrt(squares), BOUND)
    labels = lax.broadcasted_iota(jnp.int32, (USERS_MB, ROWS), 0)
    for m in range(MICRO):
        mine = u_ref[m:m + 1, :] == labels
        rows = jnp.sum(jnp.where(mine, factor[:, m:m + 1], 0.0), axis=0, keepdims=True)
        factor_ref[:, m * ROWS:(m + 1) * ROWS] = rows
    for k in range(MEMBERS):
        parts[k].wait()
        gt = gt_ref[k].reshape(DESTS * OUT, MICRO * ROWS)
        weighted = (gt.astype(jnp.float32) * factor_ref[...]).astype(jnp.bfloat16)
        if k == 0:
            inputs.wait()
        inner = x_ref[...].reshape(MICRO * ROWS, WIDTH)
        total = jnp.dot(weighted, inner, preferred_element_type=jnp.float32)
        out_ref[k] = total * (1.0 / (MICRO * NU * USERS_MB))
        writes[k].start()
    for copy in writes:
        copy.wait()


def clipped_grad(flipped, activations, row_users, squares):
    shape = (MEMBERS, DESTS * OUT, WIDTH)
    return pl.pallas_call(
        grad_kernel,
        in_specs=[
            pl.BlockSpec(memory_space=pltpu.HBM),
            pl.BlockSpec(memory_space=pltpu.HBM),
            pl.BlockSpec(memory_space=pltpu.VMEM),
            pl.BlockSpec(memory_space=pltpu.VMEM),
        ],
        out_specs=pl.BlockSpec(memory_space=pltpu.HBM),
        out_shape=jax.ShapeDtypeStruct(shape, jnp.float32),
        scratch_shapes=[
            pltpu.VMEM((MEMBERS, DESTS, OUT, MICRO * ROWS), jnp.bfloat16),
            pltpu.VMEM((MICRO, ROWS, WIDTH), jnp.bfloat16),
            pltpu.VMEM((1, MICRO * ROWS), jnp.float32),
            pltpu.VMEM(shape, jnp.float32),
            pltpu.SemaphoreType.DMA((2, MEMBERS + 1)),
        ],
        compiler_params=pltpu.CompilerParams(vmem_limit_bytes=VMEM_BYTES),
        name="grad",
    )(flipped, activations, row_users, squares)


def place(zc, xc, core):
    return ((zc + core) % NZ * NX + (xc + core) % NX) * NC + core


def stage_groups():
    first = [
        [place(2 * k + b, x, core) for b in range(2) for x in pair]
        for core in range(NC) for k in range(NZ // 2) for pair in PAIRS
    ]
    second = [
        [place(2 * k + b, x, core) for k in range(NZ // 2) for x in group]
        for core in range(NC) for b in range(2) for group in CLASSES
    ]
    return first, second


def body(activations, key_grads, row_users):
    partial = local_norms(activations, key_grads, row_users)
    squares = lax.all_to_all(partial, ("y", "core"), 0, 0)
    core = jnp.full((1,), lax.axis_index("core"), jnp.int32)
    total = clipped_grad(flip(core, key_grads), activations, row_users, squares)
    first, second = stage_groups()
    axes = ("z", "x", "core")
    total = jnp.sum(lax.all_to_all(total, axes, 0, 0, axis_index_groups=first), axis=0)
    total = total.reshape(DESTS, OUT, WIDTH)
    return jnp.sum(lax.all_to_all(total, axes, 0, 0, axis_index_groups=second), axis=0)


def solution(mesh):
    split = Mesh(mesh.devices.reshape(NZ, NX, NY, NC), ("z", "x", "y", "core"))
    user, tensor = ("z", "x"), ("y", "core")
    return jax.shard_map(
        body,
        mesh=split,
        in_specs=(P(None, user, tensor), P(None, user, None), P(None, user)),
        out_specs=P(user, tensor),
        check_vma=False,
    )
```

```python
import functools
import math

import jax
import jax.numpy as jnp
from jax import lax
from jax.experimental import pallas as pl
from jax.experimental.pallas import tpu as pltpu
from jax.sharding import Mesh, PartitionSpec as P

D = 8192
KV = 1024
MICRO = 2
ROWS = 768
USERS_MB = 8
NZ, NX, NY, NC = 8, 4, 8, 2
NU, NT = NZ * NX, NY * NC
SENT = (3, 1, 2)
CLASSES = ((0, 3), (1, 2))
MEMBERS, DESTS = 4, 8
WIDTH = D // NT
OUT = KV // NU
TILE = 256
LANES = 128
BOUND = 0.3 * math.sqrt(D * KV * ROWS / USERS_MB)
NT_DIMS = (((1,), (1,)), ((), ()))
VMEM_BYTES = 60 * 1024 * 1024


def norms_kernel(x_ref, g_ref, u_ref, out_ref):
    micro = pl.program_id(0)
    x, g = x_ref[0], g_ref[0]
    users = u_ref[pl.ds(micro, 1), :]
    columns = jnp.transpose(jnp.broadcast_to(users, (8, ROWS)))[:, :1]
    sums = []
    for first in range(0, ROWS, TILE):
        last = first + TILE
        xgram = lax.dot_general(x[:last], x[first:last], NT_DIMS, preferred_element_type=jnp.float32)
        ggram = lax.dot_general(g[:last], g[first:last], NT_DIMS, preferred_element_type=jnp.float32)
        both = jnp.where(columns[:last] == users[:, first:last], xgram * ggram, 0.0)
        total = jnp.sum(both[first:], axis=0, keepdims=True)
        if first:
            total = total + 2.0 * jnp.sum(both[:first], axis=0, keepdims=True)
        sums.append(total)
    total = jnp.concatenate(sums, axis=1)
    labels = lax.broadcasted_iota(jnp.int32, (USERS_MB, ROWS), 0)
    squares = jnp.sum(jnp.where(users == labels, total, 0.0), axis=1, keepdims=True)
    lanes = lax.broadcasted_iota(jnp.int32, (USERS_MB, LANES), 1)
    slots = lax.broadcasted_iota(jnp.int32, (USERS_MB, LANES), 0) + micro * USERS_MB
    placed = jnp.sum(jnp.where(lanes == slots, squares, 0.0), axis=0, keepdims=True)

    @pl.when(micro == 0)
    def _():
        out_ref[...] = jnp.broadcast_to(placed[None], out_ref.shape)

    @pl.when(micro != 0)
    def _():
        out_ref[...] += jnp.broadcast_to(placed[None], out_ref.shape)


def local_norms(activations, key_grads, row_users):
    return pl.pallas_call(
        norms_kernel,
        grid=(MICRO,),
        in_specs=[
            pl.BlockSpec((1, ROWS, WIDTH), lambda m: (m, 0, 0)),
            pl.BlockSpec((1, ROWS, KV), lambda m: (m, 0, 0)),
            pl.BlockSpec((MICRO, ROWS), lambda m: (0, 0)),
        ],
        out_specs=pl.BlockSpec((NT, 1, LANES), lambda m: (0, 0, 0)),
        out_shape=jax.ShapeDtypeStruct((NT, 1, LANES), jnp.float32),
        compiler_params=pltpu.CompilerParams(vmem_limit_bytes=VMEM_BYTES),
        name="norms",
    )(activations, key_grads, row_users)


def my_place():
    core = lax.axis_index("core")
    zc = lax.rem(lax.axis_index("z") + NZ - core, NZ)
    xc = lax.rem(lax.axis_index("x") + NX - core, NX)
    return core, 2 * lax.rem(zc, 2) + inner_class(xc)


def inner_class(xc):
    return jnp.where((xc == 0) | (xc == 3), 0, 1)


def flip_kernel(g_hbm, out_hbm, g_ref, out_ref, sems):
    core, own = my_place()
    reads = [pltpu.make_async_copy(g_hbm.at[m], g_ref.at[m], sems.at[0, m]) for m in range(MICRO)]
    writes = [pltpu.make_async_copy(out_ref.at[k], out_hbm.at[k], sems.at[1, k]) for k in range(MEMBERS)]
    for copy in reads:
        copy.start()
    for m in range(MICRO):
        reads[m].wait()
        for z in range(NZ):
            flipped = jnp.transpose(g_ref[m, :, z * NX * OUT:(z + 1) * NX * OUT])
            zc = lax.rem(z + NZ - core, NZ)
            for x in range(NX):
                xc = lax.rem(x + NX - core, NX)
                member = lax.bitwise_xor(2 * lax.rem(zc, 2) + inner_class(xc), own)
                dest = 2 * (zc // 2) + xc // 2
                out_ref[member, dest, :, m * ROWS:(m + 1) * ROWS] = flipped[x * OUT:(x + 1) * OUT, :]
    for copy in writes:
        copy.start()
    for copy in writes:
        copy.wait()


def flip(key_grads):
    shape = (MEMBERS, DESTS, OUT, MICRO * ROWS)
    return pl.pallas_call(
        flip_kernel,
        in_specs=[pl.BlockSpec(memory_space=pltpu.HBM)],
        out_specs=pl.BlockSpec(memory_space=pltpu.HBM),
        out_shape=jax.ShapeDtypeStruct(shape, jnp.bfloat16),
        scratch_shapes=[
            pltpu.VMEM((MICRO, ROWS, KV), jnp.bfloat16),
            pltpu.VMEM(shape, jnp.bfloat16),
            pltpu.SemaphoreType.DMA((2, MEMBERS)),
        ],
        compiler_params=pltpu.CompilerParams(vmem_limit_bytes=VMEM_BYTES),
        name="flip",
    )(key_grads)


def grad_kernel(members, gt_hbm, x_hbm, u_hbm, sq_ref, *rest):
    count = len(members)
    out_hbm = rest[:count]
    gt_ref, x_ref, u_ref, factor_ref, out_ref, sems = rest[count:]
    small = [pltpu.make_async_copy(u_hbm, u_ref, sems.at[2, 0])]
    inputs = [pltpu.make_async_copy(x_hbm.at[m], x_ref.at[m], sems.at[2, 2 + m]) for m in range(MICRO)]
    parts = [pltpu.make_async_copy(gt_hbm.at[k], gt_ref.at[at], sems.at[0, at]) for at, k in enumerate(members)]
    writes = [pltpu.make_async_copy(out_ref.at[at], out_hbm[at], sems.at[1, at]) for at in range(count)]
    for copy in small + parts[:1] + inputs + parts[1:]:
        copy.start()
    for copy in small:
        copy.wait()
    squares = jnp.sum(sq_ref[...], axis=0)
    factor = BOUND / jnp.maximum(jnp.sqrt(squares), BOUND)
    lanes = lax.broadcasted_iota(jnp.int32, (USERS_MB, LANES), 1)
    slots = lax.broadcasted_iota(jnp.int32, (USERS_MB, LANES), 0)
    labels = lax.broadcasted_iota(jnp.int32, (USERS_MB, ROWS), 0)
    for m in range(MICRO):
        column = jnp.sum(jnp.where(lanes == slots + m * USERS_MB, factor, 0.0), axis=1, keepdims=True)
        rows = jnp.sum(jnp.where(u_ref[m:m + 1, :] == labels, column, 0.0), axis=0, keepdims=True)
        factor_ref[:, m * ROWS:(m + 1) * ROWS] = rows
    for at in range(count):
        parts[at].wait()
        gt = gt_ref[at].reshape(DESTS * OUT, MICRO * ROWS)
        weighted = (gt.astype(jnp.float32) * factor_ref[...]).astype(jnp.bfloat16)
        if at == 0:
            for copy in inputs:
                copy.wait()
        inner = x_ref[...].reshape(MICRO * ROWS, WIDTH)
        total = jnp.dot(weighted, inner, preferred_element_type=jnp.float32)
        out_ref[at] = total * (1.0 / (MICRO * NU * USERS_MB))
        writes[at].start()
    for copy in writes:
        copy.wait()


def clipped_grad(members, flipped, activations, row_users, squares, vmem_bytes=VMEM_BYTES):
    count = len(members)
    shape = (DESTS * OUT, WIDTH)
    return pl.pallas_call(
        functools.partial(grad_kernel, members),
        in_specs=[pl.BlockSpec(memory_space=pltpu.HBM)] * 3 + [pl.BlockSpec(memory_space=pltpu.VMEM)],
        out_specs=[pl.BlockSpec(memory_space=pltpu.HBM)] * count,
        out_shape=[jax.ShapeDtypeStruct(shape, jnp.float32)] * count,
        scratch_shapes=[
            pltpu.VMEM((count, DESTS, OUT, MICRO * ROWS), jnp.bfloat16),
            pltpu.VMEM((MICRO, ROWS, WIDTH), jnp.bfloat16),
            pltpu.VMEM((MICRO, ROWS), jnp.int32),
            pltpu.VMEM((1, MICRO * ROWS), jnp.float32),
            pltpu.VMEM((count,) + shape, jnp.float32),
            pltpu.SemaphoreType.DMA((3, MEMBERS)),
        ],
        compiler_params=pltpu.CompilerParams(vmem_limit_bytes=vmem_bytes),
        name="grad",
    )(flipped, activations, row_users, squares)


def place(zc, xc, core):
    return ((zc + core) % NZ * NX + (xc + core) % NX) * NC + core


def stage_groups():
    first = [
        [(place(z, x, core), place(z ^ (k // 2), x ^ (k % 2), core)) for core in range(NC) for z in range(NZ) for x in range(NX)]
        for k in range(MEMBERS)
    ]
    second = [
        [place(2 * k + b, x, core) for k in range(NZ // 2) for x in group]
        for core in range(NC) for b in range(2) for group in CLASSES
    ]
    return first, second


def body(activations, key_grads, row_users):
    partial = local_norms(activations, key_grads, row_users)
    squares = lax.all_to_all(partial, ("y", "core"), 0, 0)
    flipped = flip(key_grads)
    first, second = stage_groups()
    axes = ("z", "x", "core")
    sent = clipped_grad(SENT, flipped, activations, row_users, squares, 52 * 1024 * 1024)
    kept, = clipped_grad((0,), flipped, activations, row_users, squares, 16 * 1024 * 1024)
    got = [lax.ppermute(part, axes, first[k]) for k, part in zip(SENT, sent)]
    total = kept + got[0] + got[1] + got[2]
    total = total.reshape(DESTS, OUT, WIDTH)
    return jnp.sum(lax.all_to_all(total, axes, 0, 0, axis_index_groups=second), axis=0)


def solution(mesh):
    split = Mesh(mesh.devices.reshape(NZ, NX, NY, NC), ("z", "x", "y", "core"))
    user, tensor = ("z", "x"), ("y", "core")
    return jax.shard_map(
        body,
        mesh=split,
        in_specs=(P(None, user, tensor), P(None, user, None), P(None, user)),
        out_specs=P(user, tensor),
        check_vma=False,
    )
```

```python
import functools
import math

import jax
import jax.numpy as jnp
from jax import lax
from jax.experimental import pallas as pl
from jax.experimental.pallas import tpu as pltpu
from jax.sharding import Mesh, PartitionSpec as P

D = 8192
KV = 1024
MICRO = 2
ROWS = 768
USERS_MB = 8
NZ, NX, NY, NC = 8, 4, 8, 2
NU, NT = NZ * NX, NY * NC
SENT = (3, 1, 2)
Z_CLASSES = ((0, 2, 5, 7), (1, 3, 4, 6))
X_CLASSES = ((0, 3), (1, 2))
MEMBERS, DESTS = 4, 8
WIDTH = D // NT
OUT = KV // NU
TILE = 256
LANES = 128
BOUND = 0.3 * math.sqrt(D * KV * ROWS / USERS_MB)
NT_DIMS = (((1,), (1,)), ((), ()))
VMEM_BYTES = 60 * 1024 * 1024


def norms_kernel(x_ref, g_ref, u_ref, out_ref):
    micro = pl.program_id(0)
    x, g = x_ref[0], g_ref[0]
    users = u_ref[pl.ds(micro, 1), :]
    columns = jnp.transpose(jnp.broadcast_to(users, (8, ROWS)))[:, :1]
    sums = []
    for first in range(0, ROWS, TILE):
        last = first + TILE
        xgram = lax.dot_general(x[:last], x[first:last], NT_DIMS, preferred_element_type=jnp.float32)
        ggram = lax.dot_general(g[:last], g[first:last], NT_DIMS, preferred_element_type=jnp.float32)
        both = jnp.where(columns[:last] == users[:, first:last], xgram * ggram, 0.0)
        total = jnp.sum(both[first:], axis=0, keepdims=True)
        if first:
            total = total + 2.0 * jnp.sum(both[:first], axis=0, keepdims=True)
        sums.append(total)
    total = jnp.concatenate(sums, axis=1)
    labels = lax.broadcasted_iota(jnp.int32, (USERS_MB, ROWS), 0)
    squares = jnp.sum(jnp.where(users == labels, total, 0.0), axis=1, keepdims=True)
    lanes = lax.broadcasted_iota(jnp.int32, (USERS_MB, LANES), 1)
    slots = lax.broadcasted_iota(jnp.int32, (USERS_MB, LANES), 0) + micro * USERS_MB
    placed = jnp.sum(jnp.where(lanes == slots, squares, 0.0), axis=0, keepdims=True)

    @pl.when(micro == 0)
    def _():
        out_ref[...] = jnp.broadcast_to(placed[None], out_ref.shape)

    @pl.when(micro != 0)
    def _():
        out_ref[...] += jnp.broadcast_to(placed[None], out_ref.shape)


def local_norms(activations, key_grads, row_users):
    return pl.pallas_call(
        norms_kernel,
        grid=(MICRO,),
        in_specs=[
            pl.BlockSpec((1, ROWS, WIDTH), lambda m: (m, 0, 0)),
            pl.BlockSpec((1, ROWS, KV), lambda m: (m, 0, 0)),
            pl.BlockSpec((MICRO, ROWS), lambda m: (0, 0)),
        ],
        out_specs=pl.BlockSpec((NT, 1, LANES), lambda m: (0, 0, 0)),
        out_shape=jax.ShapeDtypeStruct((NT, 1, LANES), jnp.float32),
        compiler_params=pltpu.CompilerParams(vmem_limit_bytes=VMEM_BYTES),
        name="norms",
    )(activations, key_grads, row_users)


def my_place():
    core = lax.axis_index("core")
    zc = lax.rem(lax.axis_index("z") + NZ - core, NZ)
    xc = lax.rem(lax.axis_index("x") + NX - core, NX)
    return core, class_of(zc, xc)


def class_of(zc, xc):
    along_z = lax.bitwise_xor(lax.rem(zc, 2), zc // 4)
    return 2 * along_z + jnp.where((xc == 0) | (xc == 3), 0, 1)


def flip_kernel(g_hbm, out_hbm, g_ref, out_ref, sems):
    core, own = my_place()
    reads = [pltpu.make_async_copy(g_hbm.at[m], g_ref.at[m], sems.at[0, m]) for m in range(MICRO)]
    writes = [pltpu.make_async_copy(out_ref.at[k], out_hbm.at[k], sems.at[1, k]) for k in range(MEMBERS)]
    for copy in reads:
        copy.start()
    for m in range(MICRO):
        reads[m].wait()
        for z in range(NZ):
            flipped = jnp.transpose(g_ref[m, :, z * NX * OUT:(z + 1) * NX * OUT])
            zc = lax.rem(z + NZ - core, NZ)
            for x in range(NX):
                xc = lax.rem(x + NX - core, NX)
                member = lax.bitwise_xor(class_of(zc, xc), own)
                dest = 2 * (zc // 2) + xc // 2
                out_ref[member, dest, :, m * ROWS:(m + 1) * ROWS] = flipped[x * OUT:(x + 1) * OUT, :]
    for copy in writes:
        copy.start()
    for copy in writes:
        copy.wait()


def flip(key_grads):
    shape = (MEMBERS, DESTS, OUT, MICRO * ROWS)
    return pl.pallas_call(
        flip_kernel,
        in_specs=[pl.BlockSpec(memory_space=pltpu.HBM)],
        out_specs=pl.BlockSpec(memory_space=pltpu.HBM),
        out_shape=jax.ShapeDtypeStruct(shape, jnp.bfloat16),
        scratch_shapes=[
            pltpu.VMEM((MICRO, ROWS, KV), jnp.bfloat16),
            pltpu.VMEM(shape, jnp.bfloat16),
            pltpu.SemaphoreType.DMA((2, MEMBERS)),
        ],
        compiler_params=pltpu.CompilerParams(vmem_limit_bytes=VMEM_BYTES),
        name="flip",
    )(key_grads)


def grad_kernel(members, gt_hbm, x_hbm, u_hbm, sq_ref, *rest):
    count = len(members)
    out_hbm = rest[:count]
    gt_ref, x_ref, u_ref, factor_ref, out_ref, sems = rest[count:]
    small = [pltpu.make_async_copy(u_hbm, u_ref, sems.at[2, 0])]
    inputs = [pltpu.make_async_copy(x_hbm.at[m], x_ref.at[m], sems.at[2, 2 + m]) for m in range(MICRO)]
    parts = [pltpu.make_async_copy(gt_hbm.at[k], gt_ref.at[at], sems.at[0, at]) for at, k in enumerate(members)]
    writes = [pltpu.make_async_copy(out_ref.at[at], out_hbm[at], sems.at[1, at]) for at in range(count)]
    for copy in small + parts[:1] + inputs + parts[1:]:
        copy.start()
    for copy in small:
        copy.wait()
    squares = jnp.sum(sq_ref[...], axis=0)
    factor = BOUND / jnp.maximum(jnp.sqrt(squares), BOUND)
    lanes = lax.broadcasted_iota(jnp.int32, (USERS_MB, LANES), 1)
    slots = lax.broadcasted_iota(jnp.int32, (USERS_MB, LANES), 0)
    labels = lax.broadcasted_iota(jnp.int32, (USERS_MB, ROWS), 0)
    for m in range(MICRO):
        column = jnp.sum(jnp.where(lanes == slots + m * USERS_MB, factor, 0.0), axis=1, keepdims=True)
        rows = jnp.sum(jnp.where(u_ref[m:m + 1, :] == labels, column, 0.0), axis=0, keepdims=True)
        factor_ref[:, m * ROWS:(m + 1) * ROWS] = rows
    for at in range(count):
        parts[at].wait()
        gt = gt_ref[at].reshape(DESTS * OUT, MICRO * ROWS)
        weighted = (gt.astype(jnp.float32) * factor_ref[...]).astype(jnp.bfloat16)
        if at == 0:
            for copy in inputs:
                copy.wait()
        inner = x_ref[...].reshape(MICRO * ROWS, WIDTH)
        total = jnp.dot(weighted, inner, preferred_element_type=jnp.float32)
        out_ref[at] = total * (1.0 / (MICRO * NU * USERS_MB))
        writes[at].start()
    for copy in writes:
        copy.wait()


def clipped_grad(members, flipped, activations, row_users, squares, vmem_bytes=VMEM_BYTES):
    count = len(members)
    shape = (DESTS * OUT, WIDTH)
    return pl.pallas_call(
        functools.partial(grad_kernel, members),
        in_specs=[pl.BlockSpec(memory_space=pltpu.HBM)] * 3 + [pl.BlockSpec(memory_space=pltpu.VMEM)],
        out_specs=[pl.BlockSpec(memory_space=pltpu.HBM)] * count,
        out_shape=[jax.ShapeDtypeStruct(shape, jnp.float32)] * count,
        scratch_shapes=[
            pltpu.VMEM((count, DESTS, OUT, MICRO * ROWS), jnp.bfloat16),
            pltpu.VMEM((MICRO, ROWS, WIDTH), jnp.bfloat16),
            pltpu.VMEM((MICRO, ROWS), jnp.int32),
            pltpu.VMEM((1, MICRO * ROWS), jnp.float32),
            pltpu.VMEM((count,) + shape, jnp.float32),
            pltpu.SemaphoreType.DMA((3, MEMBERS)),
        ],
        compiler_params=pltpu.CompilerParams(vmem_limit_bytes=vmem_bytes),
        name="grad",
    )(flipped, activations, row_users, squares)


def place(zc, xc, core):
    return ((zc + core) % NZ * NX + (xc + core) % NX) * NC + core


def stage_groups():
    first = [
        [(place(z, x, core), place(z ^ (k // 2), x ^ (k % 2), core)) for core in range(NC) for z in range(NZ) for x in range(NX)]
        for k in range(MEMBERS)
    ]
    second = [
        [place(z, x, core) for z in along_z for x in along_x]
        for core in range(NC) for along_z in Z_CLASSES for along_x in X_CLASSES
    ]
    return first, second


def body(activations, key_grads, row_users):
    partial = local_norms(activations, key_grads, row_users)
    squares = lax.all_to_all(partial, ("y", "core"), 0, 0)
    flipped = flip(key_grads)
    first, second = stage_groups()
    axes = ("z", "x", "core")
    sent = clipped_grad(SENT, flipped, activations, row_users, squares, 52 * 1024 * 1024)
    kept, = clipped_grad((0,), flipped, activations, row_users, squares, 16 * 1024 * 1024)
    got = [lax.ppermute(part, axes, first[k]) for k, part in zip(SENT, sent)]
    total = kept + got[0] + got[1] + got[2]
    total = total.reshape(DESTS, OUT, WIDTH)
    return jnp.sum(lax.all_to_all(total, axes, 0, 0, axis_index_groups=second), axis=0)


def solution(mesh):
    split = Mesh(mesh.devices.reshape(NZ, NX, NY, NC), ("z", "x", "y", "core"))
    user, tensor = ("z", "x"), ("y", "core")
    return jax.shard_map(
        body,
        mesh=split,
        in_specs=(P(None, user, tensor), P(None, user, None), P(None, user)),
        out_specs=P(user, tensor),
        check_vma=False,
    )
```

```python
import functools
import math

import jax
import jax.numpy as jnp
from jax import lax
from jax.experimental import pallas as pl
from jax.experimental.pallas import tpu as pltpu
from jax.sharding import Mesh, PartitionSpec as P

D = 8192
KV = 1024
MICRO = 2
ROWS = 768
USERS_MB = 8
NZ, NX, NY, NC = 8, 4, 8, 2
NU, NT = NZ * NX, NY * NC
SENT = (3, 1, 2)
Z_SHIFT = (1, 6)
X_SHIFT = (1, 0)
Z_CLASSES = ((0, 2, 5, 7), (1, 3, 4, 6))
X_CLASSES = ((0, 3), (1, 2))
MEMBERS, DESTS = 4, 8
WIDTH = D // NT
OUT = KV // NU
TILE = 256
LANES = 128
BOUND = 0.3 * math.sqrt(D * KV * ROWS / USERS_MB)
NT_DIMS = (((1,), (1,)), ((), ()))
VMEM_BYTES = 60 * 1024 * 1024


def norms_kernel(x_ref, g_ref, u_ref, out_ref):
    micro = pl.program_id(0)
    x, g = x_ref[0], g_ref[0]
    users = u_ref[pl.ds(micro, 1), :]
    columns = jnp.transpose(jnp.broadcast_to(users, (8, ROWS)))[:, :1]
    sums = []
    for first in range(0, ROWS, TILE):
        last = first + TILE
        xgram = lax.dot_general(x[:last], x[first:last], NT_DIMS, preferred_element_type=jnp.float32)
        ggram = lax.dot_general(g[:last], g[first:last], NT_DIMS, preferred_element_type=jnp.float32)
        both = jnp.where(columns[:last] == users[:, first:last], xgram * ggram, 0.0)
        total = jnp.sum(both[first:], axis=0, keepdims=True)
        if first:
            total = total + 2.0 * jnp.sum(both[:first], axis=0, keepdims=True)
        sums.append(total)
    total = jnp.concatenate(sums, axis=1)
    labels = lax.broadcasted_iota(jnp.int32, (USERS_MB, ROWS), 0)
    squares = jnp.sum(jnp.where(users == labels, total, 0.0), axis=1, keepdims=True)
    lanes = lax.broadcasted_iota(jnp.int32, (USERS_MB, LANES), 1)
    slots = lax.broadcasted_iota(jnp.int32, (USERS_MB, LANES), 0) + micro * USERS_MB
    placed = jnp.sum(jnp.where(lanes == slots, squares, 0.0), axis=0, keepdims=True)

    @pl.when(micro == 0)
    def _():
        out_ref[...] = jnp.broadcast_to(placed[None], out_ref.shape)

    @pl.when(micro != 0)
    def _():
        out_ref[...] += jnp.broadcast_to(placed[None], out_ref.shape)


def local_norms(activations, key_grads, row_users):
    return pl.pallas_call(
        norms_kernel,
        grid=(MICRO,),
        in_specs=[
            pl.BlockSpec((1, ROWS, WIDTH), lambda m: (m, 0, 0)),
            pl.BlockSpec((1, ROWS, KV), lambda m: (m, 0, 0)),
            pl.BlockSpec((MICRO, ROWS), lambda m: (0, 0)),
        ],
        out_specs=pl.BlockSpec((NT, 1, LANES), lambda m: (0, 0, 0)),
        out_shape=jax.ShapeDtypeStruct((NT, 1, LANES), jnp.float32),
        compiler_params=pltpu.CompilerParams(vmem_limit_bytes=VMEM_BYTES),
        name="norms",
    )(activations, key_grads, row_users)


def my_place():
    core = lax.axis_index("core")
    z_shift = jnp.where(core == 0, Z_SHIFT[0], Z_SHIFT[1])
    x_shift = jnp.where(core == 0, X_SHIFT[0], X_SHIFT[1])
    zc = lax.rem(lax.axis_index("z") + NZ - z_shift, NZ)
    xc = lax.rem(lax.axis_index("x") + NX - x_shift, NX)
    return z_shift, x_shift, class_of(zc, xc)


def class_of(zc, xc):
    along_z = lax.bitwise_xor(lax.rem(zc, 2), zc // 4)
    return 2 * along_z + jnp.where((xc == 0) | (xc == 3), 0, 1)


def flip_kernel(g_hbm, out_hbm, g_ref, out_ref, sems):
    z_shift, x_shift, own = my_place()
    reads = [pltpu.make_async_copy(g_hbm.at[m], g_ref.at[m], sems.at[0, m]) for m in range(MICRO)]
    writes = [pltpu.make_async_copy(out_ref.at[k], out_hbm.at[k], sems.at[1, k]) for k in range(MEMBERS)]
    for copy in reads:
        copy.start()
    for m in range(MICRO):
        reads[m].wait()
        for z in range(NZ):
            flipped = jnp.transpose(g_ref[m, :, z * NX * OUT:(z + 1) * NX * OUT])
            zc = lax.rem(z + NZ - z_shift, NZ)
            for x in range(NX):
                xc = lax.rem(x + NX - x_shift, NX)
                member = lax.bitwise_xor(class_of(zc, xc), own)
                dest = 2 * (zc // 2) + xc // 2
                out_ref[member, dest, :, m * ROWS:(m + 1) * ROWS] = flipped[x * OUT:(x + 1) * OUT, :]
    for copy in writes:
        copy.start()
    for copy in writes:
        copy.wait()


def flip(key_grads):
    shape = (MEMBERS, DESTS, OUT, MICRO * ROWS)
    return pl.pallas_call(
        flip_kernel,
        in_specs=[pl.BlockSpec(memory_space=pltpu.HBM)],
        out_specs=pl.BlockSpec(memory_space=pltpu.HBM),
        out_shape=jax.ShapeDtypeStruct(shape, jnp.bfloat16),
        scratch_shapes=[
            pltpu.VMEM((MICRO, ROWS, KV), jnp.bfloat16),
            pltpu.VMEM(shape, jnp.bfloat16),
            pltpu.SemaphoreType.DMA((2, MEMBERS)),
        ],
        compiler_params=pltpu.CompilerParams(vmem_limit_bytes=VMEM_BYTES),
        name="flip",
    )(key_grads)


def grad_kernel(members, gt_hbm, x_hbm, u_hbm, sq_ref, *rest):
    count = len(members)
    out_hbm = rest[:count]
    gt_ref, x_ref, u_ref, factor_ref, out_ref, sems = rest[count:]
    small = [pltpu.make_async_copy(u_hbm, u_ref, sems.at[2, 0])]
    inputs = [pltpu.make_async_copy(x_hbm.at[m], x_ref.at[m], sems.at[2, 2 + m]) for m in range(MICRO)]
    parts = [pltpu.make_async_copy(gt_hbm.at[k], gt_ref.at[at], sems.at[0, at]) for at, k in enumerate(members)]
    writes = [pltpu.make_async_copy(out_ref.at[at], out_hbm[at], sems.at[1, at]) for at in range(count)]
    for copy in small + parts[:1] + inputs + parts[1:]:
        copy.start()
    for copy in small:
        copy.wait()
    squares = jnp.sum(sq_ref[...], axis=0)
    factor = BOUND / jnp.maximum(jnp.sqrt(squares), BOUND)
    lanes = lax.broadcasted_iota(jnp.int32, (USERS_MB, LANES), 1)
    slots = lax.broadcasted_iota(jnp.int32, (USERS_MB, LANES), 0)
    labels = lax.broadcasted_iota(jnp.int32, (USERS_MB, ROWS), 0)
    for m in range(MICRO):
        column = jnp.sum(jnp.where(lanes == slots + m * USERS_MB, factor, 0.0), axis=1, keepdims=True)
        rows = jnp.sum(jnp.where(u_ref[m:m + 1, :] == labels, column, 0.0), axis=0, keepdims=True)
        factor_ref[:, m * ROWS:(m + 1) * ROWS] = rows
    for at in range(count):
        parts[at].wait()
        gt = gt_ref[at].reshape(DESTS * OUT, MICRO * ROWS)
        weighted = (gt.astype(jnp.float32) * factor_ref[...]).astype(jnp.bfloat16)
        if at == 0:
            for copy in inputs:
                copy.wait()
        inner = x_ref[...].reshape(MICRO * ROWS, WIDTH)
        total = jnp.dot(weighted, inner, preferred_element_type=jnp.float32)
        out_ref[at] = total * (1.0 / (MICRO * NU * USERS_MB))
        writes[at].start()
    for copy in writes:
        copy.wait()


def clipped_grad(members, flipped, activations, row_users, squares, vmem_bytes=VMEM_BYTES):
    count = len(members)
    shape = (DESTS * OUT, WIDTH)
    return pl.pallas_call(
        functools.partial(grad_kernel, members),
        in_specs=[pl.BlockSpec(memory_space=pltpu.HBM)] * 3 + [pl.BlockSpec(memory_space=pltpu.VMEM)],
        out_specs=[pl.BlockSpec(memory_space=pltpu.HBM)] * count,
        out_shape=[jax.ShapeDtypeStruct(shape, jnp.float32)] * count,
        scratch_shapes=[
            pltpu.VMEM((count, DESTS, OUT, MICRO * ROWS), jnp.bfloat16),
            pltpu.VMEM((MICRO, ROWS, WIDTH), jnp.bfloat16),
            pltpu.VMEM((MICRO, ROWS), jnp.int32),
            pltpu.VMEM((1, MICRO * ROWS), jnp.float32),
            pltpu.VMEM((count,) + shape, jnp.float32),
            pltpu.SemaphoreType.DMA((3, MEMBERS)),
        ],
        compiler_params=pltpu.CompilerParams(vmem_limit_bytes=vmem_bytes),
        name="grad",
    )(flipped, activations, row_users, squares)


def place(zc, xc, core):
    return ((zc + Z_SHIFT[core]) % NZ * NX + (xc + X_SHIFT[core]) % NX) * NC + core


def stage_groups():
    first = [
        [(place(z, x, core), place(z ^ (k // 2), x ^ (k % 2), core)) for core in range(NC) for z in range(NZ) for x in range(NX)]
        for k in range(MEMBERS)
    ]
    second = [
        [place(z, x, core) for z in along_z for x in along_x]
        for core in range(NC) for along_z in Z_CLASSES for along_x in X_CLASSES
    ]
    return first, second


def body(activations, key_grads, row_users):
    partial = local_norms(activations, key_grads, row_users)
    squares = lax.all_to_all(partial, ("y", "core"), 0, 0)
    flipped = flip(key_grads)
    first, second = stage_groups()
    axes = ("z", "x", "core")
    sent = clipped_grad(SENT, flipped, activations, row_users, squares, 52 * 1024 * 1024)
    kept, = clipped_grad((0,), flipped, activations, row_users, squares, 16 * 1024 * 1024)
    got = [lax.ppermute(part, axes, first[k]) for k, part in zip(SENT, sent)]
    total = kept + got[0] + got[1] + got[2]
    total = total.reshape(DESTS, OUT, WIDTH)
    return jnp.sum(lax.all_to_all(total, axes, 0, 0, axis_index_groups=second), axis=0)


def solution(mesh):
    split = Mesh(mesh.devices.reshape(NZ, NX, NY, NC), ("z", "x", "y", "core"))
    user, tensor = ("z", "x"), ("y", "core")
    return jax.shard_map(
        body,
        mesh=split,
        in_specs=(P(None, user, tensor), P(None, user, None), P(None, user)),
        out_specs=P(user, tensor),
        check_vma=False,
    )
```

```python
import functools
import math

import jax
import jax.numpy as jnp
from jax import lax
from jax.experimental import pallas as pl
from jax.experimental.pallas import tpu as pltpu
from jax.sharding import Mesh, PartitionSpec as P

D = 8192
KV = 1024
MICRO = 2
ROWS = 768
USERS_MB = 8
NZ, NX, NY, NC = 8, 4, 8, 2
NU, NT = NZ * NX, NY * NC
SENT = (3, 1, 2)
Z_SHIFT = (1, 6)
X_SHIFT = (1, 0)
Z_CLASSES = ((0, 2, 5, 7), (1, 3, 4, 6))
X_CLASSES = ((0, 3), (1, 2))
MEMBERS, DESTS = 4, 8
WIDTH = D // NT
OUT = KV // NU
TILE = 256
LANES = 128
BOUND = 0.3 * math.sqrt(D * KV * ROWS / USERS_MB)
NT_DIMS = (((1,), (1,)), ((), ()))
VMEM_BYTES = 60 * 1024 * 1024


def norms_kernel(x_ref, g_ref, u_ref, out_ref):
    micro = pl.program_id(0)
    x, g = x_ref[0], g_ref[0]
    users = u_ref[pl.ds(micro, 1), :]
    columns = jnp.transpose(jnp.broadcast_to(users, (8, ROWS)))[:, :1]
    sums = []
    for first in range(0, ROWS, TILE):
        last = first + TILE
        xgram = lax.dot_general(x[:last], x[first:last], NT_DIMS, preferred_element_type=jnp.float32)
        ggram = lax.dot_general(g[:last], g[first:last], NT_DIMS, preferred_element_type=jnp.float32)
        both = jnp.where(columns[:last] == users[:, first:last], xgram * ggram, 0.0)
        total = jnp.sum(both[first:], axis=0, keepdims=True)
        if first:
            total = total + 2.0 * jnp.sum(both[:first], axis=0, keepdims=True)
        sums.append(total)
    total = jnp.concatenate(sums, axis=1)
    labels = lax.broadcasted_iota(jnp.int32, (USERS_MB, ROWS), 0)
    squares = jnp.sum(jnp.where(users == labels, total, 0.0), axis=1, keepdims=True)
    lanes = lax.broadcasted_iota(jnp.int32, (USERS_MB, LANES), 1)
    slots = lax.broadcasted_iota(jnp.int32, (USERS_MB, LANES), 0) + micro * USERS_MB
    placed = jnp.sum(jnp.where(lanes == slots, squares, 0.0), axis=0, keepdims=True)

    @pl.when(micro == 0)
    def _():
        out_ref[...] = jnp.broadcast_to(placed[None], out_ref.shape)

    @pl.when(micro != 0)
    def _():
        out_ref[...] += jnp.broadcast_to(placed[None], out_ref.shape)


def local_norms(activations, key_grads, row_users):
    return pl.pallas_call(
        norms_kernel,
        grid=(MICRO,),
        in_specs=[
            pl.BlockSpec((1, ROWS, WIDTH), lambda m: (m, 0, 0)),
            pl.BlockSpec((1, ROWS, KV), lambda m: (m, 0, 0)),
            pl.BlockSpec((MICRO, ROWS), lambda m: (0, 0)),
        ],
        out_specs=pl.BlockSpec((NT, 1, LANES), lambda m: (0, 0, 0)),
        out_shape=jax.ShapeDtypeStruct((NT, 1, LANES), jnp.float32),
        compiler_params=pltpu.CompilerParams(vmem_limit_bytes=VMEM_BYTES),
        name="norms",
    )(activations, key_grads, row_users)


def my_place():
    core = lax.axis_index("core")
    z_shift = jnp.where(core == 0, Z_SHIFT[0], Z_SHIFT[1])
    x_shift = jnp.where(core == 0, X_SHIFT[0], X_SHIFT[1])
    zc = lax.rem(lax.axis_index("z") + NZ - z_shift, NZ)
    xc = lax.rem(lax.axis_index("x") + NX - x_shift, NX)
    return z_shift, x_shift, class_of(zc, xc)


def class_of(zc, xc):
    along_z = lax.bitwise_xor(lax.rem(zc, 2), zc // 4)
    return 2 * along_z + jnp.where((xc == 0) | (xc == 3), 0, 1)


def flip_kernel(g_hbm, out_hbm, g_ref, out_ref, sems):
    z_shift, x_shift, own = my_place()
    reads = [pltpu.make_async_copy(g_hbm.at[m], g_ref.at[m], sems.at[0, m]) for m in range(MICRO)]
    writes = [pltpu.make_async_copy(out_ref.at[k], out_hbm.at[k], sems.at[1, k]) for k in range(MEMBERS)]
    for copy in reads:
        copy.start()
    for m in range(MICRO):
        reads[m].wait()
        for z in range(NZ):
            flipped = jnp.transpose(g_ref[m, :, z * NX * OUT:(z + 1) * NX * OUT])
            zc = lax.rem(z + NZ - z_shift, NZ)
            for x in range(NX):
                xc = lax.rem(x + NX - x_shift, NX)
                member = lax.bitwise_xor(class_of(zc, xc), own)
                dest = 2 * (lax.rem(zc // 2, 2) * 2 + zc // 4) + xc // 2
                out_ref[member, dest, :, m * ROWS:(m + 1) * ROWS] = flipped[x * OUT:(x + 1) * OUT, :]
    for copy in writes:
        copy.start()
    for copy in writes:
        copy.wait()


def flip(key_grads):
    shape = (MEMBERS, DESTS, OUT, MICRO * ROWS)
    return pl.pallas_call(
        flip_kernel,
        in_specs=[pl.BlockSpec(memory_space=pltpu.HBM)],
        out_specs=pl.BlockSpec(memory_space=pltpu.HBM),
        out_shape=jax.ShapeDtypeStruct(shape, jnp.bfloat16),
        scratch_shapes=[
            pltpu.VMEM((MICRO, ROWS, KV), jnp.bfloat16),
            pltpu.VMEM(shape, jnp.bfloat16),
            pltpu.SemaphoreType.DMA((2, MEMBERS)),
        ],
        compiler_params=pltpu.CompilerParams(vmem_limit_bytes=VMEM_BYTES),
        name="flip",
    )(key_grads)


def grad_kernel(members, gt_hbm, x_hbm, u_hbm, sq_ref, *rest):
    count = len(members)
    out_hbm = rest[:count]
    gt_ref, x_ref, u_ref, factor_ref, out_ref, sems = rest[count:]
    small = [pltpu.make_async_copy(u_hbm, u_ref, sems.at[2, 0])]
    inputs = [pltpu.make_async_copy(x_hbm.at[m], x_ref.at[m], sems.at[2, 2 + m]) for m in range(MICRO)]
    parts = [pltpu.make_async_copy(gt_hbm.at[k], gt_ref.at[at], sems.at[0, at]) for at, k in enumerate(members)]
    writes = [pltpu.make_async_copy(out_ref.at[at], out_hbm[at], sems.at[1, at]) for at in range(count)]
    for copy in small + parts[:1] + inputs + parts[1:]:
        copy.start()
    for copy in small:
        copy.wait()
    squares = jnp.sum(sq_ref[...], axis=0)
    factor = BOUND / jnp.maximum(jnp.sqrt(squares), BOUND)
    lanes = lax.broadcasted_iota(jnp.int32, (USERS_MB, LANES), 1)
    slots = lax.broadcasted_iota(jnp.int32, (USERS_MB, LANES), 0)
    labels = lax.broadcasted_iota(jnp.int32, (USERS_MB, ROWS), 0)
    for m in range(MICRO):
        column = jnp.sum(jnp.where(lanes == slots + m * USERS_MB, factor, 0.0), axis=1, keepdims=True)
        rows = jnp.sum(jnp.where(u_ref[m:m + 1, :] == labels, column, 0.0), axis=0, keepdims=True)
        factor_ref[:, m * ROWS:(m + 1) * ROWS] = rows
    for at in range(count):
        parts[at].wait()
        gt = gt_ref[at].reshape(DESTS * OUT, MICRO * ROWS)
        weighted = (gt.astype(jnp.float32) * factor_ref[...]).astype(jnp.bfloat16)
        if at == 0:
            for copy in inputs:
                copy.wait()
        inner = x_ref[...].reshape(MICRO * ROWS, WIDTH)
        total = jnp.dot(weighted, inner, preferred_element_type=jnp.float32)
        out_ref[at] = total * (1.0 / (MICRO * NU * USERS_MB))
        writes[at].start()
    for copy in writes:
        copy.wait()


def clipped_grad(members, flipped, activations, row_users, squares, vmem_bytes=VMEM_BYTES):
    count = len(members)
    shape = (DESTS * OUT, WIDTH)
    return pl.pallas_call(
        functools.partial(grad_kernel, members),
        in_specs=[pl.BlockSpec(memory_space=pltpu.HBM)] * 3 + [pl.BlockSpec(memory_space=pltpu.VMEM)],
        out_specs=[pl.BlockSpec(memory_space=pltpu.HBM)] * count,
        out_shape=[jax.ShapeDtypeStruct(shape, jnp.float32)] * count,
        scratch_shapes=[
            pltpu.VMEM((count, DESTS, OUT, MICRO * ROWS), jnp.bfloat16),
            pltpu.VMEM((MICRO, ROWS, WIDTH), jnp.bfloat16),
            pltpu.VMEM((MICRO, ROWS), jnp.int32),
            pltpu.VMEM((1, MICRO * ROWS), jnp.float32),
            pltpu.VMEM((count,) + shape, jnp.float32),
            pltpu.SemaphoreType.DMA((3, MEMBERS)),
        ],
        compiler_params=pltpu.CompilerParams(vmem_limit_bytes=vmem_bytes),
        name="grad",
    )(flipped, activations, row_users, squares)


def place(zc, xc, core):
    return ((zc + Z_SHIFT[core]) % NZ * NX + (xc + X_SHIFT[core]) % NX) * NC + core


def stage_groups():
    first = [
        [(place(z, x, core), place(z ^ (k // 2), x ^ (k % 2), core)) for core in range(NC) for z in range(NZ) for x in range(NX)]
        for k in range(MEMBERS)
    ]
    second = [
        [place(z, x, core) for z in (along_z[i] for i in (0, 2, 1, 3)) for x in along_x]
        for core in range(NC) for along_z in Z_CLASSES for along_x in X_CLASSES
    ]
    return first, second


def body(activations, key_grads, row_users):
    partial = local_norms(activations, key_grads, row_users)
    squares = lax.all_to_all(partial, ("y", "core"), 0, 0)
    flipped = flip(key_grads)
    first, second = stage_groups()
    axes = ("z", "x", "core")
    sent = clipped_grad(SENT, flipped, activations, row_users, squares, 52 * 1024 * 1024)
    kept, = clipped_grad((0,), flipped, activations, row_users, squares, 16 * 1024 * 1024)
    got = [lax.ppermute(part, axes, first[k]) for k, part in zip(SENT, sent)]
    total = kept + got[0] + got[1] + got[2]
    total = total.reshape(DESTS, OUT, WIDTH)
    return jnp.sum(lax.all_to_all(total, axes, 0, 0, axis_index_groups=second), axis=0)


def solution(mesh):
    split = Mesh(mesh.devices.reshape(NZ, NX, NY, NC), ("z", "x", "y", "core"))
    user, tensor = ("z", "x"), ("y", "core")
    return jax.shard_map(
        body,
        mesh=split,
        in_specs=(P(None, user, tensor), P(None, user, None), P(None, user)),
        out_specs=P(user, tensor),
        check_vma=False,
    )
```

```python
import functools
import math

import jax
import jax.numpy as jnp
from jax import lax
from jax.experimental import pallas as pl
from jax.experimental.pallas import tpu as pltpu
from jax.sharding import Mesh, PartitionSpec as P

D = 8192
KV = 1024
MICRO = 2
ROWS = 768
USERS_MB = 8
NZ, NX, NY, NC = 8, 4, 8, 2
NU, NT = NZ * NX, NY * NC
SENT = (3, 2, 1)
Z_SHIFT = (1, 6)
X_SHIFT = (1, 0)
Z_CLASSES = ((0, 2, 5, 7), (1, 3, 4, 6))
X_CLASSES = ((0, 3), (1, 2))
MEMBERS, DESTS = 4, 8
WIDTH = D // NT
OUT = KV // NU
TILE = 256
LANES = 128
BOUND = 0.3 * math.sqrt(D * KV * ROWS / USERS_MB)
NT_DIMS = (((1,), (1,)), ((), ()))
VMEM_BYTES = 60 * 1024 * 1024


def norms_kernel(x_ref, g_ref, u_ref, out_ref):
    micro = pl.program_id(0)
    x, g = x_ref[0], g_ref[0]
    users = u_ref[pl.ds(micro, 1), :]
    columns = jnp.transpose(jnp.broadcast_to(users, (8, ROWS)))[:, :1]
    sums = []
    for first in range(0, ROWS, TILE):
        last = first + TILE
        xgram = lax.dot_general(x[:last], x[first:last], NT_DIMS, preferred_element_type=jnp.float32)
        ggram = lax.dot_general(g[:last], g[first:last], NT_DIMS, preferred_element_type=jnp.float32)
        both = jnp.where(columns[:last] == users[:, first:last], xgram * ggram, 0.0)
        total = jnp.sum(both[first:], axis=0, keepdims=True)
        if first:
            total = total + 2.0 * jnp.sum(both[:first], axis=0, keepdims=True)
        sums.append(total)
    total = jnp.concatenate(sums, axis=1)
    labels = lax.broadcasted_iota(jnp.int32, (USERS_MB, ROWS), 0)
    squares = jnp.sum(jnp.where(users == labels, total, 0.0), axis=1, keepdims=True)
    lanes = lax.broadcasted_iota(jnp.int32, (USERS_MB, LANES), 1)
    slots = lax.broadcasted_iota(jnp.int32, (USERS_MB, LANES), 0) + micro * USERS_MB
    placed = jnp.sum(jnp.where(lanes == slots, squares, 0.0), axis=0, keepdims=True)

    @pl.when(micro == 0)
    def _():
        out_ref[...] = jnp.broadcast_to(placed[None], out_ref.shape)

    @pl.when(micro != 0)
    def _():
        out_ref[...] += jnp.broadcast_to(placed[None], out_ref.shape)


def local_norms(activations, key_grads, row_users):
    return pl.pallas_call(
        norms_kernel,
        grid=(MICRO,),
        in_specs=[
            pl.BlockSpec((1, ROWS, WIDTH), lambda m: (m, 0, 0)),
            pl.BlockSpec((1, ROWS, KV), lambda m: (m, 0, 0)),
            pl.BlockSpec((MICRO, ROWS), lambda m: (0, 0)),
        ],
        out_specs=pl.BlockSpec((NT, 1, LANES), lambda m: (0, 0, 0)),
        out_shape=jax.ShapeDtypeStruct((NT, 1, LANES), jnp.float32),
        compiler_params=pltpu.CompilerParams(vmem_limit_bytes=VMEM_BYTES),
        name="norms",
    )(activations, key_grads, row_users)


def my_place():
    core = lax.axis_index("core")
    z_shift = jnp.where(core == 0, Z_SHIFT[0], Z_SHIFT[1])
    x_shift = jnp.where(core == 0, X_SHIFT[0], X_SHIFT[1])
    zc = lax.rem(lax.axis_index("z") + NZ - z_shift, NZ)
    xc = lax.rem(lax.axis_index("x") + NX - x_shift, NX)
    return z_shift, x_shift, class_of(zc, xc)


def class_of(zc, xc):
    along_z = lax.bitwise_xor(lax.rem(zc, 2), zc // 4)
    return 2 * along_z + jnp.where((xc == 0) | (xc == 3), 0, 1)


def flip_kernel(g_hbm, out_hbm, g_ref, out_ref, sems):
    z_shift, x_shift, own = my_place()
    reads = [pltpu.make_async_copy(g_hbm.at[m], g_ref.at[m], sems.at[0, m]) for m in range(MICRO)]
    writes = [pltpu.make_async_copy(out_ref.at[k], out_hbm.at[k], sems.at[1, k]) for k in range(MEMBERS)]
    for copy in reads:
        copy.start()
    for m in range(MICRO):
        reads[m].wait()
        for z in range(NZ):
            flipped = jnp.transpose(g_ref[m, :, z * NX * OUT:(z + 1) * NX * OUT])
            zc = lax.rem(z + NZ - z_shift, NZ)
            for x in range(NX):
                xc = lax.rem(x + NX - x_shift, NX)
                member = lax.bitwise_xor(class_of(zc, xc), own)
                dest = zc // 2 + 4 * (xc // 2)
                out_ref[member, dest, :, m * ROWS:(m + 1) * ROWS] = flipped[x * OUT:(x + 1) * OUT, :]
    for copy in writes:
        copy.start()
    for copy in writes:
        copy.wait()


def flip(key_grads):
    shape = (MEMBERS, DESTS, OUT, MICRO * ROWS)
    return pl.pallas_call(
        flip_kernel,
        in_specs=[pl.BlockSpec(memory_space=pltpu.HBM)],
        out_specs=pl.BlockSpec(memory_space=pltpu.HBM),
        out_shape=jax.ShapeDtypeStruct(shape, jnp.bfloat16),
        scratch_shapes=[
            pltpu.VMEM((MICRO, ROWS, KV), jnp.bfloat16),
            pltpu.VMEM(shape, jnp.bfloat16),
            pltpu.SemaphoreType.DMA((2, MEMBERS)),
        ],
        compiler_params=pltpu.CompilerParams(vmem_limit_bytes=VMEM_BYTES),
        name="flip",
    )(key_grads)


def grad_kernel(members, gt_hbm, x_hbm, u_hbm, sq_ref, *rest):
    count = len(members)
    out_hbm = rest[:count]
    gt_ref, x_ref, u_ref, factor_ref, out_ref, sems = rest[count:]
    small = [pltpu.make_async_copy(u_hbm, u_ref, sems.at[2, 0])]
    inputs = [pltpu.make_async_copy(x_hbm.at[m], x_ref.at[m], sems.at[2, 2 + m]) for m in range(MICRO)]
    parts = [pltpu.make_async_copy(gt_hbm.at[k], gt_ref.at[at], sems.at[0, at]) for at, k in enumerate(members)]
    writes = [pltpu.make_async_copy(out_ref.at[at], out_hbm[at], sems.at[1, at]) for at in range(count)]
    for copy in small + parts[:1] + inputs + parts[1:]:
        copy.start()
    for copy in small:
        copy.wait()
    squares = jnp.sum(sq_ref[...], axis=0)
    factor = BOUND / jnp.maximum(jnp.sqrt(squares), BOUND)
    lanes = lax.broadcasted_iota(jnp.int32, (USERS_MB, LANES), 1)
    slots = lax.broadcasted_iota(jnp.int32, (USERS_MB, LANES), 0)
    labels = lax.broadcasted_iota(jnp.int32, (USERS_MB, ROWS), 0)
    for m in range(MICRO):
        column = jnp.sum(jnp.where(lanes == slots + m * USERS_MB, factor, 0.0), axis=1, keepdims=True)
        rows = jnp.sum(jnp.where(u_ref[m:m + 1, :] == labels, column, 0.0), axis=0, keepdims=True)
        factor_ref[:, m * ROWS:(m + 1) * ROWS] = rows
    for at in range(count):
        parts[at].wait()
        gt = gt_ref[at].reshape(DESTS * OUT, MICRO * ROWS)
        weighted = (gt.astype(jnp.float32) * factor_ref[...]).astype(jnp.bfloat16)
        if at == 0:
            for copy in inputs:
                copy.wait()
        inner = x_ref[...].reshape(MICRO * ROWS, WIDTH)
        total = jnp.dot(weighted, inner, preferred_element_type=jnp.float32)
        out_ref[at] = total * (1.0 / (MICRO * NU * USERS_MB))
        writes[at].start()
    for copy in writes:
        copy.wait()


def clipped_grad(members, flipped, activations, row_users, squares, vmem_bytes=VMEM_BYTES):
    count = len(members)
    shape = (DESTS * OUT, WIDTH)
    return pl.pallas_call(
        functools.partial(grad_kernel, members),
        in_specs=[pl.BlockSpec(memory_space=pltpu.HBM)] * 3 + [pl.BlockSpec(memory_space=pltpu.VMEM)],
        out_specs=[pl.BlockSpec(memory_space=pltpu.HBM)] * count,
        out_shape=[jax.ShapeDtypeStruct(shape, jnp.float32)] * count,
        scratch_shapes=[
            pltpu.VMEM((count, DESTS, OUT, MICRO * ROWS), jnp.bfloat16),
            pltpu.VMEM((MICRO, ROWS, WIDTH), jnp.bfloat16),
            pltpu.VMEM((MICRO, ROWS), jnp.int32),
            pltpu.VMEM((1, MICRO * ROWS), jnp.float32),
            pltpu.VMEM((count,) + shape, jnp.float32),
            pltpu.SemaphoreType.DMA((3, MEMBERS)),
        ],
        compiler_params=pltpu.CompilerParams(vmem_limit_bytes=vmem_bytes),
        name="grad",
    )(flipped, activations, row_users, squares)


def place(zc, xc, core):
    return ((zc + Z_SHIFT[core]) % NZ * NX + (xc + X_SHIFT[core]) % NX) * NC + core


def stage_groups():
    first = [
        [(place(z, x, core), place(z ^ (k // 2), x ^ (k % 2), core)) for core in range(NC) for z in range(NZ) for x in range(NX)]
        for k in range(MEMBERS)
    ]
    second = [
        [place(z, x, core) for x in along_x for z in along_z]
        for core in range(NC) for along_z in Z_CLASSES for along_x in X_CLASSES
    ]
    return first, second


def body(activations, key_grads, row_users):
    partial = local_norms(activations, key_grads, row_users)
    squares = lax.all_to_all(partial, ("y", "core"), 0, 0)
    flipped = flip(key_grads)
    first, second = stage_groups()
    axes = ("z", "x", "core")
    sent = clipped_grad(SENT, flipped, activations, row_users, squares, 52 * 1024 * 1024)
    kept, = clipped_grad((0,), flipped, activations, row_users, squares, 16 * 1024 * 1024)
    got = [lax.ppermute(part, axes, first[k]) for k, part in zip(SENT, sent)]
    total = kept + got[0] + got[1] + got[2]
    total = total.reshape(DESTS, OUT, WIDTH)
    return jnp.sum(lax.all_to_all(total, axes, 0, 0, axis_index_groups=second), axis=0)


def solution(mesh):
    split = Mesh(mesh.devices.reshape(NZ, NX, NY, NC), ("z", "x", "y", "core"))
    user, tensor = ("z", "x"), ("y", "core")
    return jax.shard_map(
        body,
        mesh=split,
        in_specs=(P(None, user, tensor), P(None, user, None), P(None, user)),
        out_specs=P(user, tensor),
        check_vma=False,
    )
```

```python
import functools
import math

import jax
import jax.numpy as jnp
from jax import lax
from jax.experimental import pallas as pl
from jax.experimental.pallas import tpu as pltpu
from jax.sharding import Mesh, PartitionSpec as P

D = 8192
KV = 1024
MICRO = 2
ROWS = 768
USERS_MB = 8
NZ, NX, NY, NC = 8, 4, 8, 2
NU, NT = NZ * NX, NY * NC
SENT = (3, 2, 1)
Z_SHIFT = (1, 6)
X_SHIFT = (1, 0)
Z_CLASSES = ((0, 2, 5, 7), (1, 3, 4, 6))
X_CLASSES = ((0, 3), (1, 2))
MEMBERS, DESTS = 4, 8
WIDTH = D // NT
OUT = KV // NU
TILE = 256
LANES = 128
BOUND = 0.3 * math.sqrt(D * KV * ROWS / USERS_MB)
NT_DIMS = (((1,), (1,)), ((), ()))
VMEM_BYTES = 60 * 1024 * 1024


def norms_kernel(x_ref, g_ref, u_ref, out_ref):
    micro = pl.program_id(0)
    x, g = x_ref[0], g_ref[0]
    users = u_ref[pl.ds(micro, 1), :]
    columns = jnp.transpose(jnp.broadcast_to(users, (8, ROWS)))[:, :1]
    sums = []
    for first in range(0, ROWS, TILE):
        last = first + TILE
        xgram = lax.dot_general(x[:last], x[first:last], NT_DIMS, preferred_element_type=jnp.float32)
        ggram = lax.dot_general(g[:last], g[first:last], NT_DIMS, preferred_element_type=jnp.float32)
        both = jnp.where(columns[:last] == users[:, first:last], xgram * ggram, 0.0)
        total = jnp.sum(both[first:], axis=0, keepdims=True)
        if first:
            total = total + 2.0 * jnp.sum(both[:first], axis=0, keepdims=True)
        sums.append(total)
    total = jnp.concatenate(sums, axis=1)
    labels = lax.broadcasted_iota(jnp.int32, (USERS_MB, ROWS), 0)
    squares = jnp.sum(jnp.where(users == labels, total, 0.0), axis=1, keepdims=True)
    lanes = lax.broadcasted_iota(jnp.int32, (USERS_MB, LANES), 1)
    slots = lax.broadcasted_iota(jnp.int32, (USERS_MB, LANES), 0) + micro * USERS_MB
    placed = jnp.sum(jnp.where(lanes == slots, squares, 0.0), axis=0, keepdims=True)

    @pl.when(micro == 0)
    def _():
        out_ref[...] = jnp.broadcast_to(placed[None], out_ref.shape)

    @pl.when(micro != 0)
    def _():
        out_ref[...] += jnp.broadcast_to(placed[None], out_ref.shape)


def local_norms(activations, key_grads, row_users):
    return pl.pallas_call(
        norms_kernel,
        grid=(MICRO,),
        in_specs=[
            pl.BlockSpec((1, ROWS, WIDTH), lambda m: (m, 0, 0)),
            pl.BlockSpec((1, ROWS, KV), lambda m: (m, 0, 0)),
            pl.BlockSpec((MICRO, ROWS), lambda m: (0, 0)),
        ],
        out_specs=pl.BlockSpec((NT, 1, LANES), lambda m: (0, 0, 0)),
        out_shape=jax.ShapeDtypeStruct((NT, 1, LANES), jnp.float32),
        compiler_params=pltpu.CompilerParams(vmem_limit_bytes=VMEM_BYTES),
        name="norms",
    )(activations, key_grads, row_users)


def my_place():
    core = lax.axis_index("core")
    z_shift = jnp.where(core == 0, Z_SHIFT[0], Z_SHIFT[1])
    x_shift = jnp.where(core == 0, X_SHIFT[0], X_SHIFT[1])
    zc = lax.rem(lax.axis_index("z") + NZ - z_shift, NZ)
    xc = lax.rem(lax.axis_index("x") + NX - x_shift, NX)
    return z_shift, x_shift, class_of(zc, xc)


def class_of(zc, xc):
    along_z = lax.bitwise_xor(lax.rem(zc, 2), zc // 4)
    return 2 * along_z + jnp.where((xc == 0) | (xc == 3), 0, 1)


def flip_kernel(g_hbm, out_hbm, g_ref, out_ref, sems):
    z_shift, x_shift, own = my_place()
    reads = [pltpu.make_async_copy(g_hbm.at[m], g_ref.at[m], sems.at[0, m]) for m in range(MICRO)]
    writes = [pltpu.make_async_copy(out_ref.at[k], out_hbm.at[k], sems.at[1, k]) for k in range(MEMBERS)]
    for copy in reads:
        copy.start()
    for m in range(MICRO):
        reads[m].wait()
        for z in range(NZ):
            flipped = jnp.transpose(g_ref[m, :, z * NX * OUT:(z + 1) * NX * OUT])
            zc = lax.rem(z + NZ - z_shift, NZ)
            for x in range(NX):
                xc = lax.rem(x + NX - x_shift, NX)
                member = lax.bitwise_xor(class_of(zc, xc), own)
                dest = lax.rem(zc // 2, 2) * 2 + zc // 4 + 4 * (xc // 2)
                out_ref[member, dest, :, m * ROWS:(m + 1) * ROWS] = flipped[x * OUT:(x + 1) * OUT, :]
    for copy in writes:
        copy.start()
    for copy in writes:
        copy.wait()


def flip(key_grads):
    shape = (MEMBERS, DESTS, OUT, MICRO * ROWS)
    return pl.pallas_call(
        flip_kernel,
        in_specs=[pl.BlockSpec(memory_space=pltpu.HBM)],
        out_specs=pl.BlockSpec(memory_space=pltpu.HBM),
        out_shape=jax.ShapeDtypeStruct(shape, jnp.bfloat16),
        scratch_shapes=[
            pltpu.VMEM((MICRO, ROWS, KV), jnp.bfloat16),
            pltpu.VMEM(shape, jnp.bfloat16),
            pltpu.SemaphoreType.DMA((2, MEMBERS)),
        ],
        compiler_params=pltpu.CompilerParams(vmem_limit_bytes=VMEM_BYTES),
        name="flip",
    )(key_grads)


def grad_kernel(members, gt_hbm, x_hbm, u_hbm, sq_ref, *rest):
    count = len(members)
    out_hbm = rest[:count]
    gt_ref, x_ref, u_ref, factor_ref, out_ref, sems = rest[count:]
    small = [pltpu.make_async_copy(u_hbm, u_ref, sems.at[2, 0])]
    inputs = [pltpu.make_async_copy(x_hbm.at[m], x_ref.at[m], sems.at[2, 2 + m]) for m in range(MICRO)]
    parts = [pltpu.make_async_copy(gt_hbm.at[k], gt_ref.at[at], sems.at[0, at]) for at, k in enumerate(members)]
    writes = [pltpu.make_async_copy(out_ref.at[at], out_hbm[at], sems.at[1, at]) for at in range(count)]
    for copy in small + parts[:1] + inputs + parts[1:]:
        copy.start()
    for copy in small:
        copy.wait()
    squares = jnp.sum(sq_ref[...], axis=0)
    factor = BOUND / jnp.maximum(jnp.sqrt(squares), BOUND)
    lanes = lax.broadcasted_iota(jnp.int32, (USERS_MB, LANES), 1)
    slots = lax.broadcasted_iota(jnp.int32, (USERS_MB, LANES), 0)
    labels = lax.broadcasted_iota(jnp.int32, (USERS_MB, ROWS), 0)
    for m in range(MICRO):
        column = jnp.sum(jnp.where(lanes == slots + m * USERS_MB, factor, 0.0), axis=1, keepdims=True)
        rows = jnp.sum(jnp.where(u_ref[m:m + 1, :] == labels, column, 0.0), axis=0, keepdims=True)
        factor_ref[:, m * ROWS:(m + 1) * ROWS] = rows
    for at in range(count):
        parts[at].wait()
        gt = gt_ref[at].reshape(DESTS * OUT, MICRO * ROWS)
        weighted = (gt.astype(jnp.float32) * factor_ref[...]).astype(jnp.bfloat16)
        if at == 0:
            for copy in inputs:
                copy.wait()
        inner = x_ref[...].reshape(MICRO * ROWS, WIDTH)
        total = jnp.dot(weighted, inner, preferred_element_type=jnp.float32)
        out_ref[at] = total * (1.0 / (MICRO * NU * USERS_MB))
        writes[at].start()
    for copy in writes:
        copy.wait()


def clipped_grad(members, flipped, activations, row_users, squares, vmem_bytes=VMEM_BYTES):
    count = len(members)
    shape = (DESTS * OUT, WIDTH)
    return pl.pallas_call(
        functools.partial(grad_kernel, members),
        in_specs=[pl.BlockSpec(memory_space=pltpu.HBM)] * 3 + [pl.BlockSpec(memory_space=pltpu.VMEM)],
        out_specs=[pl.BlockSpec(memory_space=pltpu.HBM)] * count,
        out_shape=[jax.ShapeDtypeStruct(shape, jnp.float32)] * count,
        scratch_shapes=[
            pltpu.VMEM((count, DESTS, OUT, MICRO * ROWS), jnp.bfloat16),
            pltpu.VMEM((MICRO, ROWS, WIDTH), jnp.bfloat16),
            pltpu.VMEM((MICRO, ROWS), jnp.int32),
            pltpu.VMEM((1, MICRO * ROWS), jnp.float32),
            pltpu.VMEM((count,) + shape, jnp.float32),
            pltpu.SemaphoreType.DMA((3, MEMBERS)),
        ],
        compiler_params=pltpu.CompilerParams(vmem_limit_bytes=vmem_bytes),
        name="grad",
    )(flipped, activations, row_users, squares)


def place(zc, xc, core):
    return ((zc + Z_SHIFT[core]) % NZ * NX + (xc + X_SHIFT[core]) % NX) * NC + core


def stage_groups():
    first = [
        [(place(z, x, core), place(z ^ (k // 2), x ^ (k % 2), core)) for core in range(NC) for z in range(NZ) for x in range(NX)]
        for k in range(MEMBERS)
    ]
    second = [
        [place(z, x, core) for x in along_x for z in (along_z[i] for i in (0, 2, 1, 3))]
        for core in range(NC) for along_z in Z_CLASSES for along_x in X_CLASSES
    ]
    return first, second


def body(activations, key_grads, row_users):
    partial = local_norms(activations, key_grads, row_users)
    squares = lax.all_to_all(partial, ("y", "core"), 0, 0)
    flipped = flip(key_grads)
    first, second = stage_groups()
    axes = ("z", "x", "core")
    sent = clipped_grad(SENT, flipped, activations, row_users, squares, 52 * 1024 * 1024)
    kept, = clipped_grad((0,), flipped, activations, row_users, squares, 16 * 1024 * 1024)
    got = [lax.ppermute(part, axes, first[k]) for k, part in zip(SENT, sent)]
    total = kept + got[0] + got[1] + got[2]
    total = total.reshape(DESTS, OUT, WIDTH)
    return jnp.sum(lax.all_to_all(total, axes, 0, 0, axis_index_groups=second), axis=0)


def solution(mesh):
    split = Mesh(mesh.devices.reshape(NZ, NX, NY, NC), ("z", "x", "y", "core"))
    user, tensor = ("z", "x"), ("y", "core")
    return jax.shard_map(
        body,
        mesh=split,
        in_specs=(P(None, user, tensor), P(None, user, None), P(None, user)),
        out_specs=P(user, tensor),
        check_vma=False,
    )
```
